512 devices in a mesh: fsdp: 32 (over z_lo, x), seq: 16 (over y, z_hi, core).
Axes of the slice: x: 4, y: 4, z: 16 (z_hi: 2, z_lo: 8; z = z_hi * 8 + z_lo), core: 2. Of those that a mesh axis runs over, the one named last changes fastest.
Arguments:
- query: bfloat16 [65536, 4096], P(('fsdp', 'seq')), may hold values from -8 to 8
- key: bfloat16 [65536, 1024], P(('fsdp', 'seq')), may hold values from -8 to 8
- value: bfloat16 [65536, 1024], P(('fsdp', 'seq')), may hold values from -6 to 6
- out_grad: bfloat16 [65536, 4096], P(('fsdp', 'seq')), may hold values from -24 to 24
- pack_order: int32 [32, 64], P('fsdp'), may hold values from 0 to 63, each once within a row
- doc_ids: int32 [32, 1, 2048], P('fsdp'), may hold values from 0 to 3, never falling along the last dimension, each value on 1 to 1024 neighbouring positions
Outputs:
- query_grad: bfloat16 [65536, 4096], P(('fsdp', 'seq'))
- key_grad: bfloat16 [65536, 1024], P(('fsdp', 'seq'))
- value_grad: bfloat16 [65536, 1024], P(('fsdp', 'seq'))
- bias_grads: float32 [5120], P('fsdp')
The draws below stay inside these ranges and needn't reach their ends.
Inputs may be any that keep to these rules, and one draw needn't show every extreme that they name: `pack_order`: each row lists every block of its fsdp index exactly once. `doc_ids`: within a pack ids never fall; each of the 4 responses holds 1 to 1024 positions, and one holds exactly 1024.
All inputs are finite; a program needn't handle non-finite values.
Results may differ from the reference program's by a relative error of at most 0.025.
Values may be sent and summed in bfloat16 or wider, within the bound.
A program may use at most 128 MiB of HBM per device.

```python
import math
import jax
import jax.numpy as jnp
import numpy as np
from jax import lax

QH = 32
KVH = 8
HD = 128
TOK_DEV = 128
DOCS = 4
PACKS = 1
PACK_LEN = 2048
BLOCKS = 64
TOKENS = 65536
N_FSDP = 32
N_SEQ = 16


def draw_query(key, part):
    key = jax.random.fold_in(key, 11)
    drawn = jnp.clip(jax.random.normal(key, (TOKENS, QH * HD), jnp.float32), -8.0, 8.0)
    return drawn.astype(jnp.bfloat16)


def draw_key(key, part):
    key = jax.random.fold_in(key, 23)
    drawn = jnp.clip(jax.random.normal(key, (TOKENS, KVH * HD), jnp.float32), -8.0, 8.0)
    return drawn.astype(jnp.bfloat16)


def raised(values, rng, source, target, shards_of, factor):
    owner, partner = [(jnp.arange(values.shape[axis_at]) // (values.shape[axis_at] // shards_of)).reshape([-1 if axis == axis_at else 1 for axis in range(values.ndim)]) for axis_at in (source, target)]
    chosen = jax.random.permutation(rng, shards_of)[partner]
    strong = (owner == chosen) | (owner == (partner + shards_of // 2) % shards_of)
    return jnp.where(strong, factor * values, values)


def levels(rng, dims, pieces, least, top_value):
    loudness = 1.0
    for dim, blocks in pieces:
        steps = jax.random.uniform(jax.random.fold_in(jax.random.fold_in(rng, 6), dim), (blocks,), jnp.float32, least / len(pieces), top_value / len(pieces))
        loudness = loudness * jnp.repeat(jnp.exp(steps), dims[dim] // blocks).reshape((-1,) + (1,) * (len(dims) - 1 - dim))
    return loudness


def split_up(amount, total, limit, skew):
    loads = [(1 << 20) // math.isqrt(grade ** skew) + 1 for grade in range(2, amount + 1)]
    rest, counts = total - limit - (amount - 1), [1] * (amount - 1)
    while rest > 0:
        free = [i for i in range(amount - 1) if counts[i] < limit]
        pool, remaining = sum([loads[i] for i in free]), rest
        for i in free:
            extra = min(limit - counts[i], max(1, remaining * loads[i] // pool), rest)
            counts[i] = counts[i] + extra
            rest = rest - extra
    return np.array([limit] + counts)


def uneven(stream_key, amount, total, reach, slope):
    if amount == 2:
        one = jax.random.randint(stream_key, (), max(1, total - reach), min(reach, total - 1) + 1)
        return jnp.stack([one, total - one])
    tallies = jnp.asarray(split_up(amount, total, reach, slope), jnp.int32)
    pairs = (amount - 1) // 2
    donor, taker = tallies[1:1 + 2 * pairs:2], tallies[2:2 + 2 * pairs:2]
    slack = jnp.minimum(donor - 1, reach - taker)
    shifted = jax.random.randint(jax.random.fold_in(stream_key, 1), (pairs,), 0, 1 << 20) % (slack + 1)
    tallies = tallies.at[1:1 + 2 * pairs:2].set(donor - shifted).at[2:2 + 2 * pairs:2].set(taker + shifted)
    return tallies[jax.random.permutation(jax.random.fold_in(stream_key, 2), amount)]


def normal_values(rng, shape, scale, bound, cuts=(), dtype=jnp.bfloat16):
    gain = levels(rng, shape, cuts, -0.22, 0.18) if cuts else 1.0
    values = jax.random.normal(rng, shape, jnp.float32) * scale * gain
    return jnp.minimum(jnp.maximum(values, -bound), bound).astype(dtype)


def gaussian_with(key, dims, width, reach, shards, heavy, dtype=jnp.bfloat16):
    drawn = width * jax.random.normal(key, dims, jnp.float32)
    if shards:
        drawn = drawn * levels(key, dims, shards, -0.22, 0.18)
    return jnp.clip(raised(drawn, jax.random.fold_in(key, 3), *heavy), -reach, reach).astype(dtype)


def setup_inputs(seed: int = 0) -> dict:
    key_list = jax.random.split(jax.random.key(seed), 7)
    return {
        "query": draw_query(jax.random.fold_in(key_list[6], 71), 0),
        "key": draw_key(jax.random.fold_in(key_list[6], 71), 0),
        "value": normal_values(key_list[2], (TOKENS, KVH * HD), 1.0, 6.0, ((0, 512),)),
        "out_grad": gaussian_with(key_list[3], (TOKENS, QH * HD), 1.0, 24.0, ((0, 512),), (0, 1, 512, 6.0)),
        "pack_order": jax.vmap(lambda own: jax.random.permutation(own, BLOCKS))(jax.random.split(key_list[4], N_FSDP)).reshape((N_FSDP, BLOCKS)).astype(jnp.int32),
        "doc_ids": jax.vmap(lambda own: jnp.searchsorted(jnp.cumsum(uneven(own, DOCS, PACK_LEN, PACK_LEN // 2, 1)), jnp.arange(PACK_LEN), side="right"))(jax.random.split(key_list[5], N_FSDP * PACKS)).reshape((N_FSDP, PACKS, PACK_LEN)).astype(jnp.int32),
    }


def pack_rows(rows, order):
    blocks = rows.reshape((order.shape[0], -1) + rows.shape[1:])
    return jnp.take(blocks, order, axis=0).reshape(rows.shape)

def unpack_rows(rows, order):
    blocks = rows.reshape((order.shape[0], -1) + rows.shape[1:])
    restored = jnp.zeros_like(blocks).at[order].set(blocks)
    return restored.reshape(rows.shape)

def fold_parts(parts):
    repeat_factor = max(1, N_SEQ // KVH)
    parts = parts.reshape(KVH, repeat_factor, -1, PACK_LEN, HD).sum(axis=2)
    rounded = lax.optimization_barrier(parts.astype(jnp.bfloat16))
    total = rounded.astype(jnp.float32).sum(axis=1).astype(jnp.bfloat16)
    return jnp.transpose(total, (1, 0, 2))

def pack_gradients(operands):
    query_pack, key_pack, value_pack, grad_pack, doc_pack = operands
    group_size = QH // KVH
    scaling = 1.0 / math.sqrt(HD)
    key_wide = jnp.repeat(key_pack, group_size, axis=1).astype(jnp.float32)
    value_wide = jnp.repeat(value_pack, group_size, axis=1).astype(jnp.float32)
    query_wide = query_pack.astype(jnp.float32)
    grad_wide = grad_pack.astype(jnp.float32)
    positions = jnp.arange(PACK_LEN)
    allowed = (positions[None, :] <= positions[:, None]) & (doc_pack[None, :] == doc_pack[:, None])
    scores = jnp.einsum('qhd,khd->hqk', query_wide, key_wide) * scaling
    scores = jnp.where(allowed[None], scores, -1e+30)
    exponent = jnp.exp(scores - lax.optimization_barrier(jnp.max(scores, axis=-1, keepdims=True)))
    weights = lax.optimization_barrier((exponent / lax.optimization_barrier(jnp.sum(exponent, axis=-1, keepdims=True))).astype(jnp.bfloat16))
    widened = weights.astype(jnp.float32)
    prob_grad = jnp.einsum('qhd,khd->hqk', grad_wide, value_wide)
    row_dot = lax.optimization_barrier(jnp.sum(widened * prob_grad, axis=-1, keepdims=True))
    score_grad = lax.optimization_barrier((widened * (prob_grad - row_dot)).astype(jnp.bfloat16)).astype(jnp.float32)
    query_grad = (jnp.einsum('hqk,khd->qhd', score_grad, key_wide) * scaling).astype(jnp.bfloat16)
    key_parts = jnp.einsum('hqk,qhd->hkd', score_grad, query_wide) * scaling
    value_parts = jnp.einsum('hqk,qhd->hkd', widened, grad_wide)
    return (query_grad, fold_parts(key_parts), fold_parts(value_parts))

def reference(query, key, value, out_grad, pack_order, doc_ids):
    group_rows = TOK_DEV * N_SEQ

    def one_group(operands):
        query_rows, key_rows, value_rows, grad_rows, order, documents = operands

        def packed(rows, heads):
            return pack_rows(rows, order).reshape(PACKS, PACK_LEN, heads, HD)
        results = lax.map(pack_gradients, (packed(query_rows, QH), packed(key_rows, KVH), packed(value_rows, KVH), packed(grad_rows, QH), documents))
        query_back = unpack_rows(results[0].reshape(group_rows, QH * HD), order)
        key_back = unpack_rows(results[1].reshape(group_rows, KVH * HD), order)
        value_back = unpack_rows(results[2].reshape(group_rows, KVH * HD), order)
        return (query_back, key_back, value_back)
    grads = lax.map(one_group, (query.reshape(N_FSDP, group_rows, QH * HD), key.reshape(N_FSDP, group_rows, KVH * HD), value.reshape(N_FSDP, group_rows, KVH * HD), out_grad.reshape(N_FSDP, group_rows, QH * HD), pack_order, doc_ids))
    query_grad = grads[0].reshape(TOKENS, QH * HD)
    key_grad = grads[1].reshape(TOKENS, KVH * HD)
    value_grad = grads[2].reshape(TOKENS, KVH * HD)
    totals = jnp.concatenate([lax.optimization_barrier(jnp.sum(query_grad.astype(jnp.float32), axis=0)), lax.optimization_barrier(jnp.sum(value_grad.astype(jnp.float32), axis=0))])
    bias_grads = totals / math.sqrt(TOKENS)
    return (query_grad, key_grad, value_grad, bias_grads)
```

```python
import math

import jax
import jax.numpy as jnp
from jax import lax
from jax.experimental import pallas as pl
from jax.experimental.pallas import tpu as pltpu
from jax.sharding import PartitionSpec as P

QH = 32
KVH = 8
HD = 128
TOK = 128
HALF = 1024
FULL = 2048
GROUP = 4
GCOL = GROUP * HD
COLS = GROUP * HALF
TILE = 256
NX = 4
NZ = 8
BIG = 1e30
MESH = pl.DeviceIdType.MESH
F32 = jnp.float32
BF16 = jnp.bfloat16


def dot(a, b):
    return jnp.dot(a, b, preferred_element_type=F32)


def dot_nt(a, b):
    return lax.dot_general(a, b, (((1,), (1,)), ((), ())), preferred_element_type=F32)


def at128(index):
    return pl.multiple_of(index, 128)


def kernel(
    q_ref, k_ref, v_ref, g_ref, order_ref, docs_ref,
    dq_out, dk_out, dv_out, bias_out,
    qbuf, gbuf, kbuf, vbuf, km, qm, ordpad, sbuf, ebuf, gs, invl, kt, vt,
    dqb, dkb, dvb, dkl, dvl, b0, b1, b2, bl1, bl2, bl3,
    q_ss, q_rs, g_ss, g_rs, k_ss, k_rs, v_ss, v_rs,
    dq_ss, dq_rs, dk_ss, dk_rs, dv_ss, dv_rs,
    z_ss, z_rs, x_ss, x_rs, h_ss, h_rs, own_sem,
):
    f = lax.axis_index("fsdp")
    s = lax.axis_index("seq")
    x = lax.rem(f, NX)
    zl = f // NX
    y = s // 4
    zh = lax.rem(s // 2, 2)
    c = lax.rem(s, 2)
    me = y * 2 + c
    zi = zh * NZ + zl
    scaling = 1.0 / math.sqrt(HD)

    def seq_of(slot, half):
        return (slot // 2) * 4 + half * 2 + lax.rem(slot, 2)

    def remote(src, dst, ss, rs, fs, sq):
        return pltpu.make_async_remote_copy(
            src_ref=src, dst_ref=dst, send_sem=ss, recv_sem=rs,
            device_id={"fsdp": fs, "seq": sq}, device_id_type=MESH,
        )

    def repeat(low, high, body):
        def step(i, carry):
            body(i)
            return carry

        lax.fori_loop(low, high, step, 0)

    def other_slot(d):
        return lax.rem(y + d // 2, 4) * 2 + lax.rem(c + d, 2)

    def own_slot(d):
        return lax.rem(me + d, 8)

    barrier = pltpu.get_barrier_semaphore()

    def greet(fs, sq):
        pl.semaphore_signal(
            barrier, inc=1, device_id={"fsdp": fs, "seq": sq}, device_id_type=MESH
        )

    repeat(1, 16, lambda d: greet(f, lax.rem(s + d, 16)))

    def greet_line(d):
        there = lax.rem(zl + d, NZ) * NX + x
        greet(there, s)
        greet(there, seq_of(me, 1 - zh))

    repeat(1, NZ, greet_line)
    repeat(1, NX, lambda d: greet(zl * NX + lax.rem(x + d, NX), s))

    def own_copies():
        rows = pl.ds(at128(me * TOK), TOK)
        wide = pl.ds(at128(me * GCOL), GCOL)
        thin = pl.ds(at128(me * HD), HD)
        return [
            pltpu.make_async_copy(k_ref.at[:, thin], kbuf.at[rows], own_sem.at[0]),
            pltpu.make_async_copy(q_ref.at[:, wide], qbuf.at[rows], own_sem.at[1]),
            pltpu.make_async_copy(g_ref.at[:, wide], gbuf.at[rows], own_sem.at[2]),
            pltpu.make_async_copy(v_ref.at[:, thin], vbuf.at[rows], own_sem.at[3]),
        ]

    for copy in own_copies():
        copy.start()
    pl.semaphore_wait(barrier, 15 + 2 * (NZ - 1) + (NX - 1))

    def narrow_copy(src, dst, ss, rs, slot, away, sender):
        return remote(
            src.at[:, pl.ds(at128(slot * HD), HD)],
            dst.at[pl.ds(at128(away * HALF + sender * TOK), TOK)],
            ss.at[away * 8 + slot],
            rs.at[away * 8 + sender],
            f,
            seq_of(slot, zh ^ away),
        )

    def wide_copy(src, dst, ss, rs, slot, sender):
        return remote(
            src.at[:, pl.ds(at128(slot * GCOL), GCOL)],
            dst.at[pl.ds(at128(sender * TOK), TOK)],
            ss.at[slot],
            rs.at[sender],
            f,
            seq_of(slot, zh),
        )

    def k_copy(slot, away, sender):
        return narrow_copy(k_ref, kbuf, k_ss, k_rs, slot, away, sender)

    def v_copy(slot, away, sender):
        return narrow_copy(v_ref, vbuf, v_ss, v_rs, slot, away, sender)

    def q_copy(slot, sender):
        return wide_copy(q_ref, qbuf, q_ss, q_rs, slot, sender)

    def g_copy(slot, sender):
        return wide_copy(g_ref, gbuf, g_ss, g_rs, slot, sender)

    repeat(0, 8, lambda d: k_copy(other_slot(d), 1, me).start())
    repeat(1, 8, lambda d: k_copy(own_slot(d), 0, me).start())
    repeat(1, 8, lambda d: q_copy(own_slot(d), me).start())
    repeat(1, 8, lambda d: g_copy(own_slot(d), me).start())
    repeat(1, 8, lambda d: v_copy(own_slot(d), 0, me).start())

    ordpad[...] = jnp.full((8, 128), -1, jnp.int32)
    ordpad[0:1, 0:64] = order_ref[...]
    docs = docs_ref[...]
    starts = [
        jnp.sum(jnp.where(docs < d, 1.0, 0.0).astype(F32), axis=1, keepdims=True)
        for d in (1, 2, 3)
    ]

    def mask_columns(chunk):
        base = pl.multiple_of(chunk * TILE, TILE)
        row = lax.broadcasted_iota(jnp.int32, (TILE, 128), 0) + base
        lane = lax.broadcasted_iota(jnp.int32, (TILE, 128), 1)
        half = (row >> 10) ^ zh
        slot = (row >> 7) & 7
        block = (((slot >> 1) * 4 + half * 2 + (slot & 1)) << 2) + ((row >> 5) & 3)
        hot = ordpad[0:1, :] == block
        lanes = lane.astype(F32)
        place = jnp.sum(jnp.where(hot, lanes, 0.0), axis=1, keepdims=True)
        pos = place * 32.0 + (row[:, 0:1] & 31).astype(F32)
        doc = jnp.zeros((TILE, 1), F32)
        for start in starts:
            doc = doc + jnp.where(pos >= start, 1.0, 0.0)
        same = (lanes - 64.0) == doc
        first = lane < 64
        km[pl.ds(base, TILE), :] = jnp.where(
            first, jnp.where(hot, 1.0, 0.0), jnp.where(same, 1.0, 0.0)
        ).astype(BF16)

        later = jnp.where(lanes > place, -BIG, 0.0)
        differs = jnp.where(same | (lane >= 68), 0.0, -BIG)
        return jnp.where(first, later, differs).astype(BF16)

    def own_mask(chunk):
        qm[pl.ds(pl.multiple_of(chunk * TILE, TILE), TILE), :] = mask_columns(chunk)

    def other_mask(chunk):
        mask_columns(chunk)

    repeat(0, 4, own_mask)
    repeat(4, 8, other_mask)

    repeat(0, 8, lambda d: k_copy(other_slot(d), 1, me).wait_send())
    repeat(0, 8, lambda d: v_copy(other_slot(d), 1, me).start())

    own = own_copies()
    own[0].wait()
    own[1].wait()
    repeat(1, 8, lambda d: q_copy(me, own_slot(d)).wait_recv())
    repeat(1, 8, lambda d: k_copy(me, 0, own_slot(d)).wait_recv())
    repeat(0, 8, lambda d: k_copy(me, 1, other_slot(d)).wait_recv())

    tri_row = lax.broadcasted_iota(jnp.int32, (TILE, TILE), 0)
    tri_col = lax.broadcasted_iota(jnp.int32, (TILE, TILE), 1)
    triangle = jnp.where(
        ((tri_row >> 5) == (tri_col >> 5)) & (tri_row > tri_col), -BIG, 0.0
    ).astype(F32)
    nq = HALF // TILE
    nk = FULL // TILE
    exponent_scale = scaling * math.log2(math.e)

    def head_scores(head):
        lanes = pl.ds(at128(head * HD), HD)

        def query_tile(qt):
            rows = slice(qt * TILE, (qt + 1) * TILE)
            return jnp.concatenate([qbuf[rows, lanes], qm[rows, :]], axis=1)

        def score_chunk(qt, kc, q_tile, top):
            rows = slice(kc * TILE, (kc + 1) * TILE)
            k_tile = jnp.concatenate([kbuf[rows, :], km[rows, :]], axis=1)
            scores = dot_nt(k_tile, q_tile)
            if kc == qt:
                scores = scores + triangle
            sbuf[qt % 2, rows, :] = scores
            part = jnp.max(scores.reshape(TILE // 8, 8, TILE), axis=0)
            return part if top is None else jnp.maximum(top, part)

        def exp_chunk(qt, kc, top, total):
            rows = slice(kc * TILE, (kc + 1) * TILE)
            cols = pl.ds(at128(head * HALF + qt * TILE), TILE)
            exponent = jnp.exp2((sbuf[qt % 2, rows, :] - top) * exponent_scale)
            ebuf[rows, cols] = exponent.astype(BF16)
            part = jnp.sum(exponent.reshape(TILE // 8, 8, TILE), axis=0)
            return part if total is None else total + part

        tops = [None] * nq
        q_tile = query_tile(0)
        for kc in range(nk):
            tops[0] = score_chunk(0, kc, q_tile, tops[0])
        for qt in range(nq):
            top = jnp.max(tops[qt], axis=0, keepdims=True)
            total = None
            if qt + 1 < nq:
                q_tile = query_tile(qt + 1)
            for kc in range(nk):
                if qt + 1 < nq:
                    tops[qt + 1] = score_chunk(qt + 1, kc, q_tile, tops[qt + 1])
                total = exp_chunk(qt, kc, top, total)
            cols = pl.ds(at128(head * HALF + qt * TILE), TILE)
            invl[0:1, cols] = 1.0 / jnp.sum(total, axis=0, keepdims=True)

    repeat(0, GROUP, head_scores)

    own[2].wait()
    repeat(1, 8, lambda d: g_copy(me, own_slot(d)).wait_recv())

    def scale_cotangents(head):
        for qt in range(nq):
            cols = pl.ds(at128(head * HALF + qt * TILE), TILE)
            inverse = jnp.broadcast_to(invl[0:1, cols], (HD, TILE)).T
            piece = gbuf[qt * TILE : (qt + 1) * TILE, pl.ds(at128(head * HD), HD)]
            gs[cols, 0:HD] = (piece.astype(F32) * inverse).astype(BF16)

    repeat(0, GROUP, scale_cotangents)

    def back_copy(src, dst, ss, rs, slot, away, sender):
        return remote(
            src.at[pl.ds(at128(away * HALF + slot * TOK), TOK)],
            dst.at[away, sender],
            ss.at[away * 8 + slot],
            rs.at[away * 8 + sender],
            f,
            seq_of(slot, zh ^ away),
        )

    def dv_copy(slot, away, sender):
        return back_copy(dvb, dvl, dv_ss, dv_rs, slot, away, sender)

    def dk_copy(slot, away, sender):
        return back_copy(dkb, dkl, dk_ss, dk_rs, slot, away, sender)

    def value_chunk(row, sums):
        rows = pl.ds(pl.multiple_of(row, TILE), TILE)
        acc = jnp.zeros((TILE, HD), F32)
        for head in range(GROUP):
            span = slice(head * HALF, (head + 1) * HALF)
            acc = acc + dot(ebuf[rows, span], gs[span, 0:HD])
        dvb[rows, :] = acc.astype(BF16)
        return sums + jnp.sum(acc.reshape(TILE // 8, 8, HD), axis=0)

    def value_other(i, sums):
        column = lax.rem(y + i, 4)
        sums = value_chunk(HALF + column * TILE, sums)
        dv_copy(column * 2, 1, me).start()
        dv_copy(column * 2 + 1, 1, me).start()
        return sums

    sums = lax.fori_loop(0, 4, value_other, jnp.zeros((8, HD), F32))
    sums = lax.fori_loop(0, 4, lambda i, carry: value_chunk(i * TILE, carry), sums)
    repeat(1, 8, lambda d: dv_copy(own_slot(d), 0, me).start())
    b0[...] = jnp.zeros((8, 128), F32)
    b0[4:5, :] = jnp.sum(sums, axis=0, keepdims=True)

    own[3].wait()
    repeat(1, 8, lambda d: v_copy(me, 0, own_slot(d)).wait_recv())
    repeat(0, 8, lambda d: v_copy(me, 1, other_slot(d)).wait_recv())
    for chunk in range(nk):
        rows = slice(chunk * TILE, (chunk + 1) * TILE)
        vt[:, rows] = vbuf[rows, :].T
        kt[:, rows] = kbuf[rows, :].T

    lane = lax.broadcasted_iota(jnp.int32, (TILE, 128), 1)

    def row_dots(head):
        for qt in range(nq):
            cols = pl.ds(at128(head * HALF + qt * TILE), TILE)
            mixed = dot(vt[...], ebuf[:, cols]) * invl[0:1, cols]
            row_dot = jnp.sum(gs[cols, 0:HD].astype(F32) * mixed.T, axis=1, keepdims=True)
            high = row_dot.astype(BF16).astype(F32)
            rest = row_dot - high
            mid = rest.astype(BF16).astype(F32)
            low = rest - mid
            pieces = jnp.where(
                lane == 0, high, jnp.where(lane == 1, mid, jnp.where(lane == 2, low, 0.0))
            )
            gs[cols, HD : 2 * HD] = (-pieces).astype(BF16)

    repeat(0, GROUP, row_dots)

    ones = jnp.where(lane < 3, 1.0, 0.0).astype(BF16)

    def key_chunk(row):
        rows = pl.ds(pl.multiple_of(row, TILE), TILE)
        v_tile = jnp.concatenate([vbuf[rows, :], ones], axis=1)
        acc = jnp.zeros((TILE, HD), F32)
        for head in range(GROUP):
            span = slice(head * HALF, (head + 1) * HALF)
            centred = dot_nt(v_tile, gs[span, :])
            grad = centred.astype(BF16) * ebuf[rows, span]
            ebuf[rows, span] = grad
            acc = acc + dot(grad, qbuf[:, head * HD : (head + 1) * HD])
        dkb[rows, :] = (acc * scaling).astype(BF16)

    def key_other(i):
        column = lax.rem(y + i, 4)
        key_chunk(HALF + column * TILE)
        dk_copy(column * 2, 1, me).start()
        dk_copy(column * 2 + 1, 1, me).start()

    repeat(0, 4, key_other)
    repeat(0, 4, lambda i: key_chunk(i * TILE))
    repeat(1, 8, lambda d: dk_copy(own_slot(d), 0, me).start())

    def query_rows(qt, sums):
        sums = list(sums)
        for head in range(GROUP):
            cols = pl.ds(at128(head * HALF + qt * TILE), TILE)
            piece = ((dot(kt[...], ebuf[:, cols]) * scaling).T).astype(BF16)
            dqb[pl.ds(pl.multiple_of(qt * TILE, TILE), TILE), head * HD : (head + 1) * HD] = piece
            wide = piece.astype(F32).reshape(TILE // 8, 8, HD)
            sums[head] = sums[head] + jnp.sum(wide, axis=0)
        return tuple(sums)

    zero = jnp.zeros((8, HD), F32)
    q_sums = lax.fori_loop(0, nq, query_rows, (zero,) * GROUP)
    for head in range(GROUP):
        b0[head : head + 1, :] = jnp.sum(q_sums[head], axis=0, keepdims=True)

    def z_copy(d, far, target):
        there = lax.rem(zl + d, NZ)
        return remote(
            b0, bl1.at[target], z_ss.at[far * NZ + d], z_rs.at[target],
            there * NX + x, seq_of(me, zh ^ far),
        )

    def z_from(d, far):
        return z_copy(d, far, (zh ^ far) * NZ + lax.rem(zl + d, NZ))

    repeat(1, NZ, lambda d: z_copy(d, 0, zi).start())
    repeat(0, NZ, lambda d: z_copy(d, 1, zi).start())

    def dq_copy(slot, sender):
        return remote(
            dqb.at[pl.ds(at128(slot * TOK), TOK)],
            dq_out.at[:, pl.ds(at128(sender * GCOL), GCOL)],
            dq_ss.at[slot], dq_rs.at[sender], f, seq_of(slot, zh),
        )

    repeat(1, 8, lambda d: dq_copy(own_slot(d), me).start())
    own_dq = pltpu.make_async_copy(
        dqb.at[pl.ds(at128(me * TOK), TOK)],
        dq_out.at[:, pl.ds(at128(me * GCOL), GCOL)],
        own_sem.at[4],
    )
    own_dq.start()

    bl1[zi] = b0[...]
    repeat(1, NZ, lambda d: z_from(d, 0).wait_recv())
    repeat(0, NZ, lambda d: z_from(d, 1).wait_recv())
    b1[...] = jnp.sum(bl1[...], axis=0)

    def x_copy(d, target):
        return remote(
            b1, bl2.at[target], x_ss.at[d], x_rs.at[target],
            zl * NX + lax.rem(x + d, NX), s,
        )

    repeat(1, NX, lambda d: x_copy(d, x).start())
    bl2[x] = b1[...]
    repeat(1, NX, lambda d: x_copy(d, lax.rem(x + d, NX)).wait_recv())
    b2[...] = jnp.sum(bl2[...], axis=0) * (1.0 / 256.0)

    def h_copy(slot, sender):
        return remote(
            b2, bl3.at[sender], h_ss.at[slot], h_rs.at[sender], f, seq_of(slot, zh)
        )

    repeat(1, 8, lambda d: h_copy(own_slot(d), me).start())
    bl3[me] = b2[...]
    repeat(1, 8, lambda d: h_copy(me, own_slot(d)).wait_recv())
    for slot in range(8):
        bias_out[slot * 4 : slot * 4 + 4, :] = bl3[slot, 0:4, :]
        bias_out[32 + slot : 33 + slot, :] = bl3[slot, 4:5, :]

    def finish(buf, landed, copy_of, out):
        landed[0, me] = buf[pl.ds(at128(me * TOK), TOK), :]
        repeat(1, 8, lambda d: copy_of(me, 0, own_slot(d)).wait_recv())
        repeat(0, 8, lambda d: copy_of(me, 1, other_slot(d)).wait_recv())
        for slot in range(8):
            total = landed[0, slot].astype(F32) + landed[1, slot].astype(F32)
            out[:, slot * HD : (slot + 1) * HD] = total.astype(BF16)

    finish(dvb, dvl, dv_copy, dv_out)
    finish(dkb, dkl, dk_copy, dk_out)
    own_dq.wait()
    repeat(1, 8, lambda d: dq_copy(me, own_slot(d)).wait_recv())

    def near(d):
        slot = own_slot(d)
        k_copy(slot, 0, me).wait_send()
        v_copy(slot, 0, me).wait_send()
        q_copy(slot, me).wait_send()
        g_copy(slot, me).wait_send()
        dv_copy(slot, 0, me).wait_send()
        dk_copy(slot, 0, me).wait_send()
        dq_copy(slot, me).wait_send()
        h_copy(slot, me).wait_send()
        z_copy(d, 0, zi).wait_send()

    def far(d):
        slot = other_slot(d)
        v_copy(slot, 1, me).wait_send()
        dv_copy(slot, 1, me).wait_send()
        dk_copy(slot, 1, me).wait_send()
        z_copy(d, 1, zi).wait_send()

    repeat(1, 8, near)
    repeat(0, 8, far)
    repeat(1, NX, lambda d: x_copy(d, x).wait_send())


def local(query, key, value, out_grad, pack_order, doc_ids):
    vmem = pl.BlockSpec(memory_space=pltpu.VMEM)
    hbm = pl.BlockSpec(memory_space=pl.ANY)
    dma = pltpu.SemaphoreType.DMA
    query_grad, key_grad, value_grad, bias = pl.pallas_call(
        kernel,
        out_shape=(
            jax.ShapeDtypeStruct((TOK, QH * HD), BF16),
            jax.ShapeDtypeStruct((TOK, KVH * HD), BF16),
            jax.ShapeDtypeStruct((TOK, KVH * HD), BF16),
            jax.ShapeDtypeStruct((QH + KVH, HD), F32),
        ),
        in_specs=[hbm, hbm, hbm, hbm, vmem, vmem],
        out_specs=(hbm, vmem, vmem, vmem),
        scratch_shapes=[
            pltpu.VMEM((HALF, GCOL), BF16),
            pltpu.VMEM((HALF, GCOL), BF16),
            pltpu.VMEM((FULL, HD), BF16),
            pltpu.VMEM((FULL, HD), BF16),
            pltpu.VMEM((FULL, HD), BF16),
            pltpu.VMEM((HALF, HD), BF16),
            pltpu.VMEM((8, 128), jnp.int32),
            pltpu.VMEM((2, FULL, TILE), F32),
            pltpu.VMEM((FULL, COLS), BF16),
            pltpu.VMEM((COLS, 2 * HD), BF16),
            pltpu.VMEM((8, COLS), F32),
            pltpu.VMEM((HD, FULL), BF16),
            pltpu.VMEM((HD, FULL), BF16),
            pltpu.VMEM((HALF, GCOL), BF16),
            pltpu.VMEM((FULL, HD), BF16),
            pltpu.VMEM((FULL, HD), BF16),
            pltpu.VMEM((2, 8, TOK, HD), BF16),
            pltpu.VMEM((2, 8, TOK, HD), BF16),
            pltpu.VMEM((8, 128), F32),
            pltpu.VMEM((8, 128), F32),
            pltpu.VMEM((8, 128), F32),
            pltpu.VMEM((2 * NZ, 8, 128), F32),
            pltpu.VMEM((NX, 8, 128), F32),
            pltpu.VMEM((8, 8, 128), F32),
            dma((8,)), dma((8,)), dma((8,)), dma((8,)),
            dma((16,)), dma((16,)), dma((16,)), dma((16,)),
            dma((8,)), dma((8,)), dma((16,)), dma((16,)), dma((16,)), dma((16,)),
            dma((2 * NZ,)), dma((2 * NZ,)), dma((NX,)), dma((NX,)), dma((8,)), dma((8,)),
            dma((5,)),
        ],
        compiler_params=pltpu.CompilerParams(
            collective_id=0, has_side_effects=True, vmem_limit_bytes=56 << 20
        ),
        cost_estimate=pl.CostEstimate(
            flops=6 * 2 * COLS * FULL * HD, bytes_accessed=8 << 20, transcendentals=COLS * FULL
        ),
        name="attention_backward",
    )(query, key, value, out_grad, pack_order, doc_ids.reshape(1, FULL))
    width = (QH + KVH) * HD // lax.axis_size("fsdp")
    bias_grads = lax.dynamic_slice(
        bias.reshape((QH + KVH) * HD), (lax.axis_index("fsdp") * width,), (width,)
    )
    return (query_grad, key_grad, value_grad, bias_grads)


def solution(mesh):
    rows = P(("fsdp", "seq"), None)
    return jax.shard_map(
        local,
        mesh=mesh,
        in_specs=(rows, rows, rows, rows, P("fsdp", None), P("fsdp", None, None)),
        out_specs=(rows, rows, rows, P("fsdp")),
        check_vma=False,
    )
```

```python
import math

import jax
import jax.numpy as jnp
from jax import lax
from jax.experimental import pallas as pl
from jax.experimental.pallas import tpu as pltpu
from jax.sharding import PartitionSpec as P

QH = 32
KVH = 8
HD = 128
TOK = 128
HALF = 1024
FULL = 2048
GROUP = 4
GCOL = GROUP * HD
COLS = GROUP * HALF
TILE = 256
NX = 4
NZ = 8
WIDTH = (QH + KVH) * HD // (NX * NZ)
BIG = 1e30
MESH = pl.DeviceIdType.MESH
F32 = jnp.float32
BF16 = jnp.bfloat16


def dot(a, b):
    return jnp.dot(a, b, preferred_element_type=F32)


def dot_nt(a, b):
    return lax.dot_general(a, b, (((1,), (1,)), ((), ())), preferred_element_type=F32)


def at128(index):
    return pl.multiple_of(index, 128)


def kernel(
    q_ref, k_ref, v_ref, g_ref, order_ref, docs_ref,
    dq_out, dk_out, dv_out, bias_out,
    qbuf, gbuf, kbuf, vbuf, km, qm, ordpad, sbuf, ebuf, gs, invl, kt, vt,
    dqb, dkb, dvb, dkl, dvl, b0, b1, brow, bl1, bl2, bl3,
    q_ss, q_rs, g_ss, g_rs, k_ss, k_rs, v_ss, v_rs,
    dq_ss, dq_rs, dk_ss, dk_rs, dv_ss, dv_rs,
    z_ss, z_rs, x_ss, x_rs, h_ss, h_rs, own_sem,
):
    f = lax.axis_index("fsdp")
    s = lax.axis_index("seq")
    x = lax.rem(f, NX)
    zl = f // NX
    y = s // 4
    zh = lax.rem(s // 2, 2)
    c = lax.rem(s, 2)
    me = y * 2 + c
    zi = zh * NZ + zl
    scaling = 1.0 / math.sqrt(HD)

    def seq_of(slot, half):
        return (slot // 2) * 4 + half * 2 + lax.rem(slot, 2)

    def remote(src, dst, ss, rs, fs, sq):
        return pltpu.make_async_remote_copy(
            src_ref=src, dst_ref=dst, send_sem=ss, recv_sem=rs,
            device_id={"fsdp": fs, "seq": sq}, device_id_type=MESH,
        )

    def repeat(low, high, body):
        def step(i, carry):
            body(i)
            return carry

        lax.fori_loop(low, high, step, 0)

    def other_slot(d):
        return lax.rem(y + d // 2, 4) * 2 + lax.rem(c + d, 2)

    def own_slot(d):
        return lax.rem(me + d, 8)

    barrier = pltpu.get_barrier_semaphore()

    def greet(fs, sq):
        pl.semaphore_signal(
            barrier, inc=1, device_id={"fsdp": fs, "seq": sq}, device_id_type=MESH
        )

    repeat(1, 16, lambda d: greet(f, lax.rem(s + d, 16)))

    def greet_line(d):
        there = lax.rem(zl + d, NZ) * NX + x
        greet(there, s)
        greet(there, seq_of(me, 1 - zh))

    repeat(1, NZ, greet_line)
    repeat(1, NX, lambda d: greet(zl * NX + lax.rem(x + d, NX), s))

    def own_copies():
        rows = pl.ds(at128(me * TOK), TOK)
        wide = pl.ds(at128(me * GCOL), GCOL)
        thin = pl.ds(at128(me * HD), HD)
        return [
            pltpu.make_async_copy(k_ref.at[:, thin], kbuf.at[rows], own_sem.at[0]),
            pltpu.make_async_copy(q_ref.at[:, wide], qbuf.at[rows], own_sem.at[1]),
            pltpu.make_async_copy(g_ref.at[:, wide], gbuf.at[rows], own_sem.at[2]),
            pltpu.make_async_copy(v_ref.at[:, thin], vbuf.at[rows], own_sem.at[3]),
        ]

    for copy in own_copies():
        copy.start()
    pl.semaphore_wait(barrier, 15 + 2 * (NZ - 1) + (NX - 1))

    def narrow_copy(src, dst, ss, rs, slot, away, sender):
        return remote(
            src.at[:, pl.ds(at128(slot * HD), HD)],
            dst.at[pl.ds(at128(away * HALF + sender * TOK), TOK)],
            ss.at[away * 8 + slot],
            rs.at[away * 8 + sender],
            f,
            seq_of(slot, zh ^ away),
        )

    def wide_copy(src, dst, ss, rs, slot, sender):
        return remote(
            src.at[:, pl.ds(at128(slot * GCOL), GCOL)],
            dst.at[pl.ds(at128(sender * TOK), TOK)],
            ss.at[slot],
            rs.at[sender],
            f,
            seq_of(slot, zh),
        )

    def k_copy(slot, away, sender):
        return narrow_copy(k_ref, kbuf, k_ss, k_rs, slot, away, sender)

    def v_copy(slot, away, sender):
        return narrow_copy(v_ref, vbuf, v_ss, v_rs, slot, away, sender)

    def q_copy(slot, sender):
        return wide_copy(q_ref, qbuf, q_ss, q_rs, slot, sender)

    def g_copy(slot, sender):
        return wide_copy(g_ref, gbuf, g_ss, g_rs, slot, sender)

    repeat(0, 8, lambda d: k_copy(other_slot(d), 1, me).start())
    repeat(1, 8, lambda d: k_copy(own_slot(d), 0, me).start())
    repeat(1, 8, lambda d: q_copy(own_slot(d), me).start())

    ordpad[...] = jnp.full((8, 128), -1, jnp.int32)
    ordpad[0:1, 0:64] = order_ref[...]
    docs = docs_ref[...]
    starts = [
        jnp.sum(jnp.where(docs < d, 1.0, 0.0).astype(F32), axis=1, keepdims=True)
        for d in (1, 2, 3)
    ]

    def mask_columns(chunk):
        base = pl.multiple_of(chunk * TILE, TILE)
        row = lax.broadcasted_iota(jnp.int32, (TILE, 128), 0) + base
        lane = lax.broadcasted_iota(jnp.int32, (TILE, 128), 1)
        half = (row >> 10) ^ zh
        slot = (row >> 7) & 7
        block = (((slot >> 1) * 4 + half * 2 + (slot & 1)) << 2) + ((row >> 5) & 3)
        hot = ordpad[0:1, :] == block
        lanes = lane.astype(F32)
        place = jnp.sum(jnp.where(hot, lanes, 0.0), axis=1, keepdims=True)
        pos = place * 32.0 + (row[:, 0:1] & 31).astype(F32)
        doc = jnp.zeros((TILE, 1), F32)
        for start in starts:
            doc = doc + jnp.where(pos >= start, 1.0, 0.0)
        same = (lanes - 64.0) == doc
        first = lane < 64
        km[pl.ds(base, TILE), :] = jnp.where(
            first, jnp.where(hot, 1.0, 0.0), jnp.where(same, 1.0, 0.0)
        ).astype(BF16)

        later = jnp.where(lanes > place, -BIG, 0.0)
        differs = jnp.where(same | (lane >= 68), 0.0, -BIG)
        return jnp.where(first, later, differs).astype(BF16)

    def own_mask(chunk):
        qm[pl.ds(pl.multiple_of(chunk * TILE, TILE), TILE), :] = mask_columns(chunk)

    def other_mask(chunk):
        mask_columns(chunk)

    repeat(0, 4, own_mask)
    repeat(4, 8, other_mask)

    def value_send(d):
        k_copy(other_slot(d), 1, me).wait_send()
        v_copy(other_slot(d), 1, me).start()

    repeat(0, 8, value_send)
    repeat(1, 8, lambda d: g_copy(own_slot(d), me).start())
    repeat(1, 8, lambda d: v_copy(own_slot(d), 0, me).start())

    own = own_copies()
    own[0].wait()
    own[1].wait()
    repeat(1, 8, lambda d: q_copy(me, own_slot(d)).wait_recv())
    repeat(1, 8, lambda d: k_copy(me, 0, own_slot(d)).wait_recv())
    repeat(0, 8, lambda d: k_copy(me, 1, other_slot(d)).wait_recv())

    tri_row = lax.broadcasted_iota(jnp.int32, (TILE, TILE), 0)
    tri_col = lax.broadcasted_iota(jnp.int32, (TILE, TILE), 1)
    triangle = jnp.where(
        ((tri_row >> 5) == (tri_col >> 5)) & (tri_row > tri_col), -BIG, 0.0
    ).astype(F32)
    nq = HALF // TILE
    nk = FULL // TILE
    exponent_scale = scaling * math.log2(math.e)

    def head_scores(head):
        lanes = pl.ds(at128(head * HD), HD)

        def query_tile(qt):
            rows = slice(qt * TILE, (qt + 1) * TILE)
            return jnp.concatenate([qbuf[rows, lanes], qm[rows, :]], axis=1)

        def score_chunk(qt, kc, q_tile, top):
            rows = slice(kc * TILE, (kc + 1) * TILE)
            k_tile = jnp.concatenate([kbuf[rows, :], km[rows, :]], axis=1)
            scores = dot_nt(k_tile, q_tile)
            if kc == qt:
                scores = scores + triangle
            sbuf[qt % 2, rows, :] = scores
            part = jnp.max(scores.reshape(TILE // 8, 8, TILE), axis=0)
            return part if top is None else jnp.maximum(top, part)

        def exp_chunk(qt, kc, top, total):
            rows = slice(kc * TILE, (kc + 1) * TILE)
            cols = pl.ds(at128(head * HALF + qt * TILE), TILE)
            exponent = jnp.exp2((sbuf[qt % 2, rows, :] - top) * exponent_scale)
            ebuf[rows, cols] = exponent.astype(BF16)
            part = jnp.sum(exponent.reshape(TILE // 8, 8, TILE), axis=0)
            return part if total is None else total + part

        tops = [None] * nq
        q_tile = query_tile(0)
        for kc in range(nk):
            tops[0] = score_chunk(0, kc, q_tile, tops[0])
        for qt in range(nq):
            top = jnp.max(tops[qt], axis=0, keepdims=True)
            total = None
            if qt + 1 < nq:
                q_tile = query_tile(qt + 1)
            for kc in range(nk):
                if qt + 1 < nq:
                    tops[qt + 1] = score_chunk(qt + 1, kc, q_tile, tops[qt + 1])
                total = exp_chunk(qt, kc, top, total)
            cols = pl.ds(at128(head * HALF + qt * TILE), TILE)
            invl[0:1, cols] = 1.0 / jnp.sum(total, axis=0, keepdims=True)

    repeat(0, GROUP, head_scores)

    own[2].wait()
    repeat(1, 8, lambda d: g_copy(me, own_slot(d)).wait_recv())

    def scale_cotangents(head):
        for qt in range(nq):
            cols = pl.ds(at128(head * HALF + qt * TILE), TILE)
            inverse = jnp.broadcast_to(invl[0:1, cols], (HD, TILE)).T
            piece = gbuf[qt * TILE : (qt + 1) * TILE, pl.ds(at128(head * HD), HD)]
            gs[cols, 0:HD] = (piece.astype(F32) * inverse).astype(BF16)

    repeat(0, GROUP, scale_cotangents)

    def back_copy(src, dst, ss, rs, slot, away, sender):
        return remote(
            src.at[pl.ds(at128(away * HALF + slot * TOK), TOK)],
            dst.at[away, sender],
            ss.at[away * 8 + slot],
            rs.at[away * 8 + sender],
            f,
            seq_of(slot, zh ^ away),
        )

    def dv_copy(slot, away, sender):
        return back_copy(dvb, dvl, dv_ss, dv_rs, slot, away, sender)

    def dk_copy(slot, away, sender):
        return back_copy(dkb, dkl, dk_ss, dk_rs, slot, away, sender)

    def value_chunk(row, sums):
        rows = pl.ds(pl.multiple_of(row, TILE), TILE)
        acc = jnp.zeros((TILE, HD), F32)
        for head in range(GROUP):
            span = slice(head * HALF, (head + 1) * HALF)
            acc = acc + dot(ebuf[rows, span], gs[span, 0:HD])
        dvb[rows, :] = acc.astype(BF16)
        return sums + jnp.sum(acc.reshape(TILE // 8, 8, HD), axis=0)

    def value_other(i, sums):
        column = lax.rem(y + i, 4)
        sums = value_chunk(HALF + column * TILE, sums)
        dv_copy(column * 2, 1, me).start()
        dv_copy(column * 2 + 1, 1, me).start()
        return sums

    sums = lax.fori_loop(0, 4, value_other, jnp.zeros((8, HD), F32))
    sums = lax.fori_loop(0, 4, lambda i, carry: value_chunk(i * TILE, carry), sums)
    repeat(1, 8, lambda d: dv_copy(own_slot(d), 0, me).start())
    b0[...] = jnp.zeros((8, 128), F32)
    b0[4:5, :] = jnp.sum(sums, axis=0, keepdims=True)

    own[3].wait()
    repeat(1, 8, lambda d: v_copy(me, 0, own_slot(d)).wait_recv())
    repeat(0, 8, lambda d: v_copy(me, 1, other_slot(d)).wait_recv())
    for chunk in range(nk):
        rows = slice(chunk * TILE, (chunk + 1) * TILE)
        vt[:, rows] = vbuf[rows, :].T
        kt[:, rows] = kbuf[rows, :].T

    lane = lax.broadcasted_iota(jnp.int32, (TILE, 128), 1)

    def row_dots(head):
        for qt in range(nq):
            cols = pl.ds(at128(head * HALF + qt * TILE), TILE)
            mixed = dot(vt[...], ebuf[:, cols]) * invl[0:1, cols]
            row_dot = jnp.sum(gs[cols, 0:HD].astype(F32) * mixed.T, axis=1, keepdims=True)
            high = row_dot.astype(BF16).astype(F32)
            rest = row_dot - high
            mid = rest.astype(BF16).astype(F32)
            low = rest - mid
            pieces = jnp.where(
                lane == 0, high, jnp.where(lane == 1, mid, jnp.where(lane == 2, low, 0.0))
            )
            gs[cols, HD : 2 * HD] = (-pieces).astype(BF16)

    repeat(0, GROUP, row_dots)

    ones = jnp.where(lane < 3, 1.0, 0.0).astype(BF16)

    def score_gradients(i):
        rows = pl.ds(pl.multiple_of(i * TILE, TILE), TILE)
        v_tile = jnp.concatenate([vbuf[rows, :], ones], axis=1)
        for head in range(GROUP):
            span = slice(head * HALF, (head + 1) * HALF)
            centred = dot_nt(v_tile, gs[span, :])
            ebuf[rows, span] = centred.astype(BF16) * ebuf[rows, span]

    repeat(0, nk, score_gradients)

    def query_rows(qt, sums):
        sums = list(sums)
        for head in range(GROUP):
            cols = pl.ds(at128(head * HALF + qt * TILE), TILE)
            piece = ((dot(kt[...], ebuf[:, cols]) * scaling).T).astype(BF16)
            dqb[pl.ds(pl.multiple_of(qt * TILE, TILE), TILE), head * HD : (head + 1) * HD] = piece
            wide = piece.astype(F32).reshape(TILE // 8, 8, HD)
            sums[head] = sums[head] + jnp.sum(wide, axis=0)
        return tuple(sums)

    zero = jnp.zeros((8, HD), F32)
    q_sums = lax.fori_loop(0, nq, query_rows, (zero,) * GROUP)
    for head in range(GROUP):
        b0[head : head + 1, :] = jnp.sum(q_sums[head], axis=0, keepdims=True)

    def x_copy(d, target):
        return remote(
            b0, bl1.at[target], x_ss.at[d], x_rs.at[target],
            zl * NX + lax.rem(x + d, NX), s,
        )

    repeat(1, NX, lambda d: x_copy(d, x).start())
    bl1[x] = b0[...]
    repeat(1, NX, lambda d: x_copy(d, lax.rem(x + d, NX)).wait_recv())
    b1[...] = jnp.sum(bl1[...], axis=0) * (1.0 / 256.0)

    def h_copy(slot, sender):
        return remote(
            b1, bl2.at[sender], h_ss.at[slot], h_rs.at[sender], f, seq_of(slot, zh)
        )

    repeat(1, 8, lambda d: h_copy(own_slot(d), me).start())
    bl2[me] = b1[...]
    repeat(1, 8, lambda d: h_copy(me, own_slot(d)).wait_recv())
    for slot in range(8):
        for head in range(GROUP):
            brow[slot * GROUP + head] = bl2[slot, head : head + 1, :]
        brow[QH + slot] = bl2[slot, 4:5, :]

    def z_copy(d, far, target):
        there = lax.rem(zl + d, NZ) * NX + x
        return remote(
            brow.at[pl.ds((there * WIDTH) // HD, 2)], bl3.at[target],
            z_ss.at[far * NZ + d], z_rs.at[target], there, seq_of(me, zh ^ far),
        )

    def z_from(d, far):
        return z_copy(d, far, (zh ^ far) * NZ + lax.rem(zl + d, NZ))

    repeat(0, NZ, lambda d: z_copy(d, 1, zi).start())
    repeat(1, NZ, lambda d: z_copy(d, 0, zi).start())

    def key_chunk(row):
        rows = pl.ds(pl.multiple_of(row, TILE), TILE)
        acc = jnp.zeros((TILE, HD), F32)
        for head in range(GROUP):
            span = slice(head * HALF, (head + 1) * HALF)
            acc = acc + dot(ebuf[rows, span], qbuf[:, head * HD : (head + 1) * HD])
        dkb[rows, :] = (acc * scaling).astype(BF16)

    def key_other(i):
        column = lax.rem(y + i, 4)
        key_chunk(HALF + column * TILE)
        dk_copy(column * 2, 1, me).start()
        dk_copy(column * 2 + 1, 1, me).start()

    repeat(0, 4, key_other)

    def dq_copy(slot, sender):
        return remote(
            dqb.at[pl.ds(at128(slot * TOK), TOK)],
            dq_out.at[:, pl.ds(at128(sender * GCOL), GCOL)],
            dq_ss.at[slot], dq_rs.at[sender], f, seq_of(slot, zh),
        )

    repeat(1, 8, lambda d: dq_copy(own_slot(d), me).start())
    own_dq = pltpu.make_async_copy(
        dqb.at[pl.ds(at128(me * TOK), TOK)],
        dq_out.at[:, pl.ds(at128(me * GCOL), GCOL)],
        own_sem.at[4],
    )
    own_dq.start()
    repeat(0, 4, lambda i: key_chunk(i * TILE))
    repeat(1, 8, lambda d: dk_copy(own_slot(d), 0, me).start())

    def finish(buf, landed, copy_of, out):
        landed[0, me] = buf[pl.ds(at128(me * TOK), TOK), :]
        repeat(1, 8, lambda d: copy_of(me, 0, own_slot(d)).wait_recv())
        repeat(0, 8, lambda d: copy_of(me, 1, other_slot(d)).wait_recv())
        for slot in range(8):
            total = landed[0, slot].astype(F32) + landed[1, slot].astype(F32)
            out[:, slot * HD : (slot + 1) * HD] = total.astype(BF16)

    finish(dvb, dvl, dv_copy, dv_out)
    bl3[zi] = brow[pl.ds((f * WIDTH) // HD, 2)]
    repeat(1, NZ, lambda d: z_from(d, 0).wait_recv())
    repeat(0, NZ, lambda d: z_from(d, 1).wait_recv())
    total = jnp.sum(bl3[...], axis=0)
    bias_out[0:1, :] = total[0]
    bias_out[1:2, :] = total[1]
    finish(dkb, dkl, dk_copy, dk_out)
    own_dq.wait()
    repeat(1, 8, lambda d: dq_copy(me, own_slot(d)).wait_recv())

    def near(d):
        slot = own_slot(d)
        k_copy(slot, 0, me).wait_send()
        v_copy(slot, 0, me).wait_send()
        q_copy(slot, me).wait_send()
        g_copy(slot, me).wait_send()
        dv_copy(slot, 0, me).wait_send()
        dk_copy(slot, 0, me).wait_send()
        dq_copy(slot, me).wait_send()
        h_copy(slot, me).wait_send()
        z_copy(d, 0, zi).wait_send()

    def far(d):
        slot = other_slot(d)
        v_copy(slot, 1, me).wait_send()
        dv_copy(slot, 1, me).wait_send()
        dk_copy(slot, 1, me).wait_send()
        z_copy(d, 1, zi).wait_send()

    repeat(1, 8, near)
    repeat(0, 8, far)
    repeat(1, NX, lambda d: x_copy(d, x).wait_send())


def place(f_dq, f_dk, f_dv, f_bias, dq_out, dk_out, dv_out, bias_out):
    dq_out[...] = f_dq[...]
    dk_out[...] = f_dk[...]
    dv_out[...] = f_dv[...]
    first = lax.axis_index("fsdp") * WIDTH
    pair = jnp.concatenate([f_bias[0:1, :], f_bias[1:2, :]], axis=1)
    shift = lax.rem(first, HD)
    piece = pair[:, 0:WIDTH]
    for step in range(1, 4):
        start = step * (HD // 4)
        piece = jnp.where(shift == start, pair[:, start : start + WIDTH], piece)
    bias_out[...] = piece


def local(query, key, value, out_grad, pack_order, doc_ids):
    vmem = pl.BlockSpec(memory_space=pltpu.VMEM)
    hbm = pl.BlockSpec(memory_space=pl.ANY)
    dma = pltpu.SemaphoreType.DMA
    query_grad, key_grad, value_grad, bias = pl.pallas_call(
        kernel,
        out_shape=(
            jax.ShapeDtypeStruct((TOK, QH * HD), BF16),
            jax.ShapeDtypeStruct((TOK, KVH * HD), BF16),
            jax.ShapeDtypeStruct((TOK, KVH * HD), BF16),
            jax.ShapeDtypeStruct((2, HD), F32),
        ),
        in_specs=[hbm, hbm, hbm, hbm, vmem, vmem],
        out_specs=(hbm, vmem, vmem, vmem),
        scratch_shapes=[
            pltpu.VMEM((HALF, GCOL), BF16),
            pltpu.VMEM((HALF, GCOL), BF16),
            pltpu.VMEM((FULL, HD), BF16),
            pltpu.VMEM((FULL, HD), BF16),
            pltpu.VMEM((FULL, HD), BF16),
            pltpu.VMEM((HALF, HD), BF16),
            pltpu.VMEM((8, 128), jnp.int32),
            pltpu.VMEM((2, FULL, TILE), F32),
            pltpu.VMEM((FULL, COLS), BF16),
            pltpu.VMEM((COLS, 2 * HD), BF16),
            pltpu.VMEM((8, COLS), F32),
            pltpu.VMEM((HD, FULL), BF16),
            pltpu.VMEM((HD, FULL), BF16),
            pltpu.VMEM((HALF, GCOL), BF16),
            pltpu.VMEM((FULL, HD), BF16),
            pltpu.VMEM((FULL, HD), BF16),
            pltpu.VMEM((2, 8, TOK, HD), BF16),
            pltpu.VMEM((2, 8, TOK, HD), BF16),
            pltpu.VMEM((8, 128), F32),
            pltpu.VMEM((8, 128), F32),
            pltpu.VMEM((QH + KVH, 1, HD), F32),
            pltpu.VMEM((NX, 8, 128), F32),
            pltpu.VMEM((8, 8, 128), F32),
            pltpu.VMEM((2 * NZ, 2, 1, HD), F32),
            dma((8,)), dma((8,)), dma((8,)), dma((8,)),
            dma((16,)), dma((16,)), dma((16,)), dma((16,)),
            dma((8,)), dma((8,)), dma((16,)), dma((16,)), dma((16,)), dma((16,)),
            dma((2 * NZ,)), dma((2 * NZ,)), dma((NX,)), dma((NX,)), dma((8,)), dma((8,)),
            dma((5,)),
        ],
        compiler_params=pltpu.CompilerParams(
            collective_id=0, has_side_effects=True, vmem_limit_bytes=56 << 20
        ),
        cost_estimate=pl.CostEstimate(
            flops=6 * 2 * COLS * FULL * HD, bytes_accessed=8 << 20, transcendentals=COLS * FULL
        ),
        name="attention_backward",
    )(query, key, value, out_grad, pack_order, doc_ids.reshape(1, FULL))
    query_grad, key_grad, value_grad, bias_grads = pl.pallas_call(
        place,
        out_shape=(
            jax.ShapeDtypeStruct((TOK, QH * HD), BF16),
            jax.ShapeDtypeStruct((TOK, KVH * HD), BF16),
            jax.ShapeDtypeStruct((TOK, KVH * HD), BF16),
            jax.ShapeDtypeStruct((1, WIDTH), F32),
        ),
        in_specs=[vmem] * 4,
        out_specs=(vmem,) * 4,
        name="place_gradients",
    )(query_grad, key_grad, value_grad, bias)
    bias_grads = bias_grads.reshape(WIDTH)
    return (query_grad, key_grad, value_grad, bias_grads)


def solution(mesh):
    rows = P(("fsdp", "seq"), None)
    return jax.shard_map(
        local,
        mesh=mesh,
        in_specs=(rows, rows, rows, rows, P("fsdp", None), P("fsdp", None, None)),
        out_specs=(rows, rows, rows, P("fsdp")),
        check_vma=False,
    )
```

```python
import math

import jax
import jax.numpy as jnp
from jax import lax
from jax.experimental import pallas as pl
from jax.experimental.pallas import tpu as pltpu
from jax.sharding import PartitionSpec as P

QH = 32
KVH = 8
HD = 128
TOK = 128
HALF = 1024
FULL = 2048
GROUP = 4
GCOL = GROUP * HD
COLS = GROUP * HALF
TILE = 256
NX = 4
NZ = 8
WIDTH = (QH + KVH) * HD // (NX * NZ)
BIG = 1e30
MESH = pl.DeviceIdType.MESH
F32 = jnp.float32
BF16 = jnp.bfloat16


def dot(a, b):
    return jnp.dot(a, b, preferred_element_type=F32)


def dot_nt(a, b):
    return lax.dot_general(a, b, (((1,), (1,)), ((), ())), preferred_element_type=F32)


def at128(index):
    return pl.multiple_of(index, 128)


def kernel(
    q_ref, k_ref, v_ref, g_ref, order_ref, docs_ref,
    dq_out, dk_out, dv_out, bias_out,
    qbuf, gbuf, kbuf, vbuf, km, qm, ordpad, sbuf, ebuf, gs, invl, kt, vt,
    dqb, dkb, dvb, dkl, dvl, b0, b1, brow, bl1, bl2, bl3,
    q_ss, q_rs, g_ss, g_rs, k_ss, k_rs, v_ss, v_rs,
    dq_ss, dq_rs, dk_ss, dk_rs, dv_ss, dv_rs,
    z_ss, z_rs, x_ss, x_rs, h_ss, h_rs, own_sem,
):
    f = lax.axis_index("fsdp")
    s = lax.axis_index("seq")
    x = lax.rem(f, NX)
    zl = f // NX
    y = s // 4
    zh = lax.rem(s // 2, 2)
    c = lax.rem(s, 2)
    me = y * 2 + c
    zi = zh * NZ + zl
    scaling = 1.0 / math.sqrt(HD)

    def seq_of(slot, half):
        return (slot // 2) * 4 + half * 2 + lax.rem(slot, 2)

    def remote(src, dst, ss, rs, fs, sq):
        return pltpu.make_async_remote_copy(
            src_ref=src, dst_ref=dst, send_sem=ss, recv_sem=rs,
            device_id={"fsdp": fs, "seq": sq}, device_id_type=MESH,
        )

    def repeat(low, high, body):
        def step(i, carry):
            body(i)
            return carry

        lax.fori_loop(low, high, step, 0)

    def other_slot(d):
        return lax.rem(y + d // 2, 4) * 2 + lax.rem(c + d, 2)

    def own_slot(d):
        return lax.rem(me + d, 8)

    barrier = pltpu.get_barrier_semaphore()

    def greet(fs, sq):
        pl.semaphore_signal(
            barrier, inc=1, device_id={"fsdp": fs, "seq": sq}, device_id_type=MESH
        )

    repeat(1, 16, lambda d: greet(f, lax.rem(s + d, 16)))

    def greet_line(d):
        there = lax.rem(zl + d, NZ) * NX + x
        greet(there, s)
        greet(there, seq_of(me, 1 - zh))

    repeat(1, NZ, greet_line)
    repeat(1, NX, lambda d: greet(zl * NX + lax.rem(x + d, NX), s))

    def own_copies():
        rows = pl.ds(at128(me * TOK), TOK)
        wide = pl.ds(at128(me * GCOL), GCOL)
        thin = pl.ds(at128(me * HD), HD)
        return [
            pltpu.make_async_copy(k_ref.at[:, thin], kbuf.at[rows], own_sem.at[0]),
            pltpu.make_async_copy(q_ref.at[:, wide], qbuf.at[rows], own_sem.at[1]),
            pltpu.make_async_copy(g_ref.at[:, wide], gbuf.at[rows], own_sem.at[2]),
            pltpu.make_async_copy(v_ref.at[:, thin], vbuf.at[rows], own_sem.at[3]),
        ]

    for copy in own_copies():
        copy.start()
    pl.semaphore_wait(barrier, 15 + 2 * (NZ - 1) + (NX - 1))

    def narrow_copy(src, dst, ss, rs, slot, away, sender):
        return remote(
            src.at[:, pl.ds(at128(slot * HD), HD)],
            dst.at[pl.ds(at128(away * HALF + sender * TOK), TOK)],
            ss.at[away * 8 + slot],
            rs.at[away * 8 + sender],
            f,
            seq_of(slot, zh ^ away),
        )

    def wide_copy(src, dst, ss, rs, slot, sender):
        return remote(
            src.at[:, pl.ds(at128(slot * GCOL), GCOL)],
            dst.at[pl.ds(at128(sender * TOK), TOK)],
            ss.at[slot],
            rs.at[sender],
            f,
            seq_of(slot, zh),
        )

    def k_copy(slot, away, sender):
        return narrow_copy(k_ref, kbuf, k_ss, k_rs, slot, away, sender)

    def v_copy(slot, away, sender):
        return narrow_copy(v_ref, vbuf, v_ss, v_rs, slot, away, sender)

    def q_copy(slot, sender):
        return wide_copy(q_ref, qbuf, q_ss, q_rs, slot, sender)

    def g_copy(slot, sender):
        return wide_copy(g_ref, gbuf, g_ss, g_rs, slot, sender)

    repeat(0, 8, lambda d: k_copy(other_slot(d), 1, me).start())
    repeat(1, 8, lambda d: k_copy(own_slot(d), 0, me).start())
    repeat(1, 8, lambda d: q_copy(own_slot(d), me).start())

    ordpad[...] = jnp.full((8, 128), -1, jnp.int32)
    ordpad[0:1, 0:64] = order_ref[...]
    docs = docs_ref[...]
    starts = [
        jnp.sum(jnp.where(docs < d, 1.0, 0.0).astype(F32), axis=1, keepdims=True)
        for d in (1, 2, 3)
    ]

    def mask_columns(chunk):
        base = pl.multiple_of(chunk * TILE, TILE)
        row = lax.broadcasted_iota(jnp.int32, (TILE, 128), 0) + base
        lane = lax.broadcasted_iota(jnp.int32, (TILE, 128), 1)
        half = (row >> 10) ^ zh
        slot = (row >> 7) & 7
        block = (((slot >> 1) * 4 + half * 2 + (slot & 1)) << 2) + ((row >> 5) & 3)
        hot = ordpad[0:1, :] == block
        lanes = lane.astype(F32)
        place = jnp.sum(jnp.where(hot, lanes, 0.0), axis=1, keepdims=True)
        pos = place * 32.0 + (row[:, 0:1] & 31).astype(F32)
        doc = jnp.zeros((TILE, 1), F32)
        for start in starts:
            doc = doc + jnp.where(pos >= start, 1.0, 0.0)
        same = (lanes - 64.0) == doc
        first = lane < 64
        km[pl.ds(base, TILE), :] = jnp.where(
            first, jnp.where(hot, 1.0, 0.0), jnp.where(same, 1.0, 0.0)
        ).astype(BF16)

        later = jnp.where(lanes > place, -BIG, 0.0)
        differs = jnp.where(same | (lane >= 68), 0.0, -BIG)
        return jnp.where(first, later, differs).astype(BF16)

    def own_mask(chunk):
        qm[pl.ds(pl.multiple_of(chunk * TILE, TILE), TILE), :] = mask_columns(chunk)

    def other_mask(chunk):
        mask_columns(chunk)

    repeat(0, 4, own_mask)
    repeat(4, 8, other_mask)

    def value_send(d):
        k_copy(other_slot(d), 1, me).wait_send()
        v_copy(other_slot(d), 1, me).start()

    repeat(0, 8, value_send)
    repeat(1, 8, lambda d: g_copy(own_slot(d), me).start())
    repeat(1, 8, lambda d: v_copy(own_slot(d), 0, me).start())

    own = own_copies()
    own[0].wait()
    own[1].wait()
    repeat(1, 8, lambda d: q_copy(me, own_slot(d)).wait_recv())
    repeat(1, 8, lambda d: k_copy(me, 0, own_slot(d)).wait_recv())
    repeat(0, 8, lambda d: k_copy(me, 1, other_slot(d)).wait_recv())

    tri_row = lax.broadcasted_iota(jnp.int32, (TILE, TILE), 0)
    tri_col = lax.broadcasted_iota(jnp.int32, (TILE, TILE), 1)
    triangle = jnp.where(
        ((tri_row >> 5) == (tri_col >> 5)) & (tri_row > tri_col), -BIG, 0.0
    ).astype(F32)
    nq = HALF // TILE
    nk = FULL // TILE
    exponent_scale = scaling * math.log2(math.e)

    def head_scores(head):
        lanes = pl.ds(at128(head * HD), HD)

        def query_tile(qt):
            rows = slice(qt * TILE, (qt + 1) * TILE)
            return jnp.concatenate([qbuf[rows, lanes], qm[rows, :]], axis=1)

        def score_chunk(qt, kc, q_tile, top):
            rows = slice(kc * TILE, (kc + 1) * TILE)
            k_tile = jnp.concatenate([kbuf[rows, :], km[rows, :]], axis=1)
            scores = dot_nt(k_tile, q_tile)
            if kc == qt:
                scores = scores + triangle
            sbuf[qt % 2, rows, :] = scores
            part = jnp.max(scores.reshape(TILE // 8, 8, TILE), axis=0)
            return part if top is None else jnp.maximum(top, part)

        def exp_chunk(qt, kc, top, total):
            rows = slice(kc * TILE, (kc + 1) * TILE)
            cols = pl.ds(at128(head * HALF + qt * TILE), TILE)
            exponent = jnp.exp2((sbuf[qt % 2, rows, :] - top) * exponent_scale)
            ebuf[rows, cols] = exponent.astype(BF16)
            part = jnp.sum(exponent.reshape(TILE // 8, 8, TILE), axis=0)
            return part if total is None else total + part

        tops = [None] * nq
        q_tile = query_tile(0)
        for kc in range(nk):
            tops[0] = score_chunk(0, kc, q_tile, tops[0])
        for qt in range(nq):
            top = jnp.max(tops[qt], axis=0, keepdims=True)
            total = None
            if qt + 1 < nq:
                q_tile = query_tile(qt + 1)
            for kc in range(nk):
                if qt + 1 < nq:
                    tops[qt + 1] = score_chunk(qt + 1, kc, q_tile, tops[qt + 1])
                total = exp_chunk(qt, kc, top, total)
            cols = pl.ds(at128(head * HALF + qt * TILE), TILE)
            invl[0:1, cols] = 1.0 / jnp.sum(total, axis=0, keepdims=True)

    repeat(0, GROUP, head_scores)

    own[2].wait()
    repeat(1, 8, lambda d: g_copy(me, own_slot(d)).wait_recv())

    def scale_cotangents(head):
        for qt in range(nq):
            cols = pl.ds(at128(head * HALF + qt * TILE), TILE)
            inverse = jnp.broadcast_to(invl[0:1, cols], (HD, TILE)).T
            piece = gbuf[qt * TILE : (qt + 1) * TILE, pl.ds(at128(head * HD), HD)]
            gs[cols, 0:HD] = (piece.astype(F32) * inverse).astype(BF16)

    repeat(0, GROUP, scale_cotangents)

    def back_copy(src, dst, ss, rs, slot, away, sender):
        return remote(
            src.at[pl.ds(at128(away * HALF + slot * TOK), TOK)],
            dst.at[away, sender],
            ss.at[away * 8 + slot],
            rs.at[away * 8 + sender],
            f,
            seq_of(slot, zh ^ away),
        )

    def dv_copy(slot, away, sender):
        return back_copy(dvb, dvl, dv_ss, dv_rs, slot, away, sender)

    def dk_copy(slot, away, sender):
        return back_copy(dkb, dkl, dk_ss, dk_rs, slot, away, sender)

    def value_chunk(row, sums):
        rows = pl.ds(pl.multiple_of(row, TILE), TILE)
        acc = jnp.zeros((TILE, HD), F32)
        for head in range(GROUP):
            span = slice(head * HALF, (head + 1) * HALF)
            acc = acc + dot(ebuf[rows, span], gs[span, 0:HD])
        dvb[rows, :] = acc.astype(BF16)
        return sums + jnp.sum(acc.reshape(TILE // 8, 8, HD), axis=0)

    def value_other(i, sums):
        column = lax.rem(y + i, 4)
        sums = value_chunk(HALF + column * TILE, sums)
        dv_copy(column * 2, 1, me).start()
        dv_copy(column * 2 + 1, 1, me).start()
        return sums

    sums = lax.fori_loop(0, 4, value_other, jnp.zeros((8, HD), F32))
    sums = lax.fori_loop(0, 4, lambda i, carry: value_chunk(i * TILE, carry), sums)
    repeat(1, 8, lambda d: dv_copy(own_slot(d), 0, me).start())
    b0[...] = jnp.zeros((8, 128), F32)
    b0[4:5, :] = jnp.sum(sums, axis=0, keepdims=True)

    own[3].wait()
    repeat(1, 8, lambda d: v_copy(me, 0, own_slot(d)).wait_recv())
    repeat(0, 8, lambda d: v_copy(me, 1, other_slot(d)).wait_recv())
    for chunk in range(nk):
        rows = slice(chunk * TILE, (chunk + 1) * TILE)
        vt[:, rows] = vbuf[rows, :].T
        kt[:, rows] = kbuf[rows, :].T

    lane = lax.broadcasted_iota(jnp.int32, (TILE, 128), 1)

    def row_dots(head):
        for qt in range(nq):
            cols = pl.ds(at128(head * HALF + qt * TILE), TILE)
            mixed = dot(vt[...], ebuf[:, cols]) * invl[0:1, cols]
            row_dot = jnp.sum(gs[cols, 0:HD].astype(F32) * mixed.T, axis=1, keepdims=True)
            high = row_dot.astype(BF16).astype(F32)
            rest = row_dot - high
            mid = rest.astype(BF16).astype(F32)
            low = rest - mid
            pieces = jnp.where(
                lane == 0, high, jnp.where(lane == 1, mid, jnp.where(lane == 2, low, 0.0))
            )
            gs[cols, HD : 2 * HD] = (-pieces).astype(BF16)

    repeat(0, GROUP, row_dots)

    ones = jnp.where(lane < 3, 1.0, 0.0).astype(BF16)

    def score_gradients(i):
        rows = pl.ds(pl.multiple_of(i * TILE, TILE), TILE)
        v_tile = jnp.concatenate([vbuf[rows, :], ones], axis=1)
        for head in range(GROUP):
            span = slice(head * HALF, (head + 1) * HALF)
            centred = dot_nt(v_tile, gs[span, :])
            ebuf[rows, span] = centred.astype(BF16) * ebuf[rows, span]

    repeat(0, nk, score_gradients)

    def query_rows(qt, sums):
        sums = list(sums)
        for head in range(GROUP):
            cols = pl.ds(at128(head * HALF + qt * TILE), TILE)
            piece = ((dot(kt[...], ebuf[:, cols]) * scaling).T).astype(BF16)
            dqb[pl.ds(pl.multiple_of(qt * TILE, TILE), TILE), head * HD : (head + 1) * HD] = piece
            wide = piece.astype(F32).reshape(TILE // 8, 8, HD)
            sums[head] = sums[head] + jnp.sum(wide, axis=0)
        return tuple(sums)

    zero = jnp.zeros((8, HD), F32)
    q_sums = lax.fori_loop(0, nq, query_rows, (zero,) * GROUP)
    for head in range(GROUP):
        b0[head : head + 1, :] = jnp.sum(q_sums[head], axis=0, keepdims=True)

    def x_copy(d, target):
        return remote(
            b0, bl1.at[target], x_ss.at[d], x_rs.at[target],
            zl * NX + lax.rem(x + d, NX), s,
        )

    repeat(1, NX, lambda d: x_copy(d, x).start())
    bl1[x] = b0[...]
    repeat(1, NX, lambda d: x_copy(d, lax.rem(x + d, NX)).wait_recv())
    b1[...] = jnp.sum(bl1[...], axis=0) * (1.0 / 256.0)

    def h_copy(slot, sender):
        return remote(
            b1, bl2.at[sender], h_ss.at[slot], h_rs.at[sender], f, seq_of(slot, zh)
        )

    repeat(1, 8, lambda d: h_copy(own_slot(d), me).start())
    bl2[me] = b1[...]
    repeat(1, 8, lambda d: h_copy(me, own_slot(d)).wait_recv())
    for slot in range(8):
        for head in range(GROUP):
            brow[slot * GROUP + head] = bl2[slot, head : head + 1, :]
        brow[QH + slot] = bl2[slot, 4:5, :]

    def z_copy(d, far, target):
        there = lax.rem(zl + d, NZ) * NX + x
        return remote(
            brow.at[pl.ds((there * WIDTH) // HD, 2)], bl3.at[target],
            z_ss.at[far * NZ + d], z_rs.at[target], there, seq_of(me, zh ^ far),
        )

    def z_from(d, far):
        return z_copy(d, far, (zh ^ far) * NZ + lax.rem(zl + d, NZ))

    repeat(0, NZ, lambda d: z_copy(d, 1, zi).start())
    repeat(1, NZ, lambda d: z_copy(d, 0, zi).start())

    def key_chunk(row):
        rows = pl.ds(pl.multiple_of(row, TILE), TILE)
        acc = jnp.zeros((TILE, HD), F32)
        for head in range(GROUP):
            span = slice(head * HALF, (head + 1) * HALF)
            acc = acc + dot(ebuf[rows, span], qbuf[:, head * HD : (head + 1) * HD])
        dkb[rows, :] = (acc * scaling).astype(BF16)

    def key_other(i):
        column = lax.rem(y + i, 4)
        key_chunk(HALF + column * TILE)
        dk_copy(column * 2, 1, me).start()
        dk_copy(column * 2 + 1, 1, me).start()

    repeat(0, 4, key_other)

    def dq_copy(slot, sender):
        return remote(
            dqb.at[pl.ds(at128(slot * TOK), TOK)],
            dq_out.at[:, pl.ds(at128(sender * GCOL), GCOL)],
            dq_ss.at[slot], dq_rs.at[sender], f, seq_of(slot, zh),
        )

    repeat(1, 8, lambda d: dq_copy(own_slot(d), me).start())
    own_dq = pltpu.make_async_copy(
        dqb.at[pl.ds(at128(me * TOK), TOK)],
        dq_out.at[:, pl.ds(at128(me * GCOL), GCOL)],
        own_sem.at[4],
    )
    own_dq.start()
    repeat(0, 4, lambda i: key_chunk(i * TILE))
    repeat(1, 8, lambda d: dk_copy(own_slot(d), 0, me).start())

    def finish(buf, landed, copy_of, out):
        landed[0, me] = buf[pl.ds(at128(me * TOK), TOK), :]
        for d in range(8):
            slot = own_slot(d)
            if d:
                copy_of(me, 0, slot).wait_recv()
            copy_of(me, 1, slot).wait_recv()
            total = landed[0, slot].astype(F32) + landed[1, slot].astype(F32)
            out[:, pl.ds(at128(slot * HD), HD)] = total.astype(BF16)

    finish(dvb, dvl, dv_copy, dv_out)
    bl3[zi] = brow[pl.ds((f * WIDTH) // HD, 2)]
    repeat(1, NZ, lambda d: z_from(d, 0).wait_recv())
    repeat(0, NZ, lambda d: z_from(d, 1).wait_recv())
    total = jnp.sum(bl3[...], axis=0)
    bias_out[0:1, :] = total[0]
    bias_out[1:2, :] = total[1]
    own_dq.wait()
    repeat(1, 8, lambda d: dq_copy(me, own_slot(d)).wait_recv())

    def near(d):
        slot = own_slot(d)
        k_copy(slot, 0, me).wait_send()
        v_copy(slot, 0, me).wait_send()
        q_copy(slot, me).wait_send()
        g_copy(slot, me).wait_send()
        dv_copy(slot, 0, me).wait_send()
        dk_copy(slot, 0, me).wait_send()
        dq_copy(slot, me).wait_send()
        h_copy(slot, me).wait_send()
        z_copy(d, 0, zi).wait_send()

    def far(d):
        slot = other_slot(d)
        v_copy(slot, 1, me).wait_send()
        dv_copy(slot, 1, me).wait_send()
        dk_copy(slot, 1, me).wait_send()
        z_copy(d, 1, zi).wait_send()

    repeat(1, 8, near)
    repeat(0, 8, far)
    repeat(1, NX, lambda d: x_copy(d, x).wait_send())

    finish(dkb, dkl, dk_copy, dk_out)


def place(f_dq, f_dk, f_dv, f_bias, dq_out, dk_out, dv_out, bias_out):
    dq_out[...] = f_dq[...]
    dk_out[...] = f_dk[...]
    dv_out[...] = f_dv[...]
    first = lax.axis_index("fsdp") * WIDTH
    pair = jnp.concatenate([f_bias[0:1, :], f_bias[1:2, :]], axis=1)
    shift = lax.rem(first, HD)
    piece = pair[:, 0:WIDTH]
    for step in range(1, 4):
        start = step * (HD // 4)
        piece = jnp.where(shift == start, pair[:, start : start + WIDTH], piece)
    bias_out[...] = piece


def local(query, key, value, out_grad, pack_order, doc_ids):
    vmem = pl.BlockSpec(memory_space=pltpu.VMEM)
    hbm = pl.BlockSpec(memory_space=pl.ANY)
    dma = pltpu.SemaphoreType.DMA
    query_grad, key_grad, value_grad, bias = pl.pallas_call(
        kernel,
        out_shape=(
            jax.ShapeDtypeStruct((TOK, QH * HD), BF16),
            jax.ShapeDtypeStruct((TOK, KVH * HD), BF16),
            jax.ShapeDtypeStruct((TOK, KVH * HD), BF16),
            jax.ShapeDtypeStruct((2, HD), F32),
        ),
        in_specs=[hbm, hbm, hbm, hbm, vmem, vmem],
        out_specs=(hbm, vmem, vmem, vmem),
        scratch_shapes=[
            pltpu.VMEM((HALF, GCOL), BF16),
            pltpu.VMEM((HALF, GCOL), BF16),
            pltpu.VMEM((FULL, HD), BF16),
            pltpu.VMEM((FULL, HD), BF16),
            pltpu.VMEM((FULL, HD), BF16),
            pltpu.VMEM((HALF, HD), BF16),
            pltpu.VMEM((8, 128), jnp.int32),
            pltpu.VMEM((2, FULL, TILE), F32),
            pltpu.VMEM((FULL, COLS), BF16),
            pltpu.VMEM((COLS, 2 * HD), BF16),
            pltpu.VMEM((8, COLS), F32),
            pltpu.VMEM((HD, FULL), BF16),
            pltpu.VMEM((HD, FULL), BF16),
            pltpu.VMEM((HALF, GCOL), BF16),
            pltpu.VMEM((FULL, HD), BF16),
            pltpu.VMEM((FULL, HD), BF16),
            pltpu.VMEM((2, 8, TOK, HD), BF16),
            pltpu.VMEM((2, 8, TOK, HD), BF16),
            pltpu.VMEM((8, 128), F32),
            pltpu.VMEM((8, 128), F32),
            pltpu.VMEM((QH + KVH, 1, HD), F32),
            pltpu.VMEM((NX, 8, 128), F32),
            pltpu.VMEM((8, 8, 128), F32),
            pltpu.VMEM((2 * NZ, 2, 1, HD), F32),
            dma((8,)), dma((8,)), dma((8,)), dma((8,)),
            dma((16,)), dma((16,)), dma((16,)), dma((16,)),
            dma((8,)), dma((8,)), dma((16,)), dma((16,)), dma((16,)), dma((16,)),
            dma((2 * NZ,)), dma((2 * NZ,)), dma((NX,)), dma((NX,)), dma((8,)), dma((8,)),
            dma((5,)),
        ],
        compiler_params=pltpu.CompilerParams(
            collective_id=0, has_side_effects=True, vmem_limit_bytes=56 << 20
        ),
        cost_estimate=pl.CostEstimate(
            flops=6 * 2 * COLS * FULL * HD, bytes_accessed=8 << 20, transcendentals=COLS * FULL
        ),
        name="attention_backward",
    )(query, key, value, out_grad, pack_order, doc_ids.reshape(1, FULL))
    query_grad, key_grad, value_grad, bias_grads = pl.pallas_call(
        place,
        out_shape=(
            jax.ShapeDtypeStruct((TOK, QH * HD), BF16),
            jax.ShapeDtypeStruct((TOK, KVH * HD), BF16),
            jax.ShapeDtypeStruct((TOK, KVH * HD), BF16),
            jax.ShapeDtypeStruct((1, WIDTH), F32),
        ),
        in_specs=[vmem] * 4,
        out_specs=(vmem,) * 4,
        name="place_gradients",
    )(query_grad, key_grad, value_grad, bias)
    bias_grads = bias_grads.reshape(WIDTH)
    return (query_grad, key_grad, value_grad, bias_grads)


def solution(mesh):
    rows = P(("fsdp", "seq"), None)
    return jax.shard_map(
        local,
        mesh=mesh,
        in_specs=(rows, rows, rows, rows, P("fsdp", None), P("fsdp", None, None)),
        out_specs=(rows, rows, rows, P("fsdp")),
        check_vma=False,
    )
```
